32 devices in a mesh: group: 2 (over x), expert: 8 (over z, y), tensor: 2 (over core).
Axes of the slice: x: 2, y: 2, z: 4, core: 2. Of those that a mesh axis runs over, the one named last changes fastest.
Arguments:
- tokens: bfloat16 [2048, 4096], P(('group', 'expert'), 'tensor'), parts along dimension 0, may hold values from -6 to 6
- latent_down: bfloat16 [4096, 1024], P('tensor'), may hold values from -0.09375 to 0.09375
- expert_gate: bfloat16 [8, 1024, 2048], P('expert', None, 'tensor'), may hold values from -0.1875 to 0.1875
- expert_up: bfloat16 [8, 1024, 2048], P('expert', None, 'tensor'), may hold values from -0.1875 to 0.1875
- expert_down: bfloat16 [8, 2048, 1024], P('expert', 'tensor'), may hold values from -0.125 to 0.125
- routes: int32 [2048, 4], P(('group', 'expert')), parts along dimension 0, may hold values from 0 to 7, all different within a row; in each aligned block of 128 rows (0 to 127, 128 to 255, ...) at most 128 rows name the same one
- gates: float32 [2048, 4], P(('group', 'expert')), parts along dimension 0, may hold values from 0.1 to 1
Outputs:
- mixed: bfloat16 [2048, 1024], P(('group', 'expert'), 'tensor'), parts along dimension 0
The draws below stay inside these ranges and needn't reach their ends.
There are 2 independent parts, one for each index of `group`. The reference program is written for one: setup_inputs(seed, part) draws one part's arguments, and reference() takes and returns one part's arrays. A program takes and returns all parts, laid end to end along the dimension named above; an argument that names none is the same for every part. Nothing has to cross between parts.
Inputs may be any that keep to these rules, and one draw needn't show every extreme that they name: `routes`: the 4 experts of a row differ. The rows of one aligned block of 128 name one expert at most 128 times, and in every draw some block names some expert exactly 128 times.
All inputs are finite; a program needn't handle non-finite values.
Results may differ from the reference program's by a relative error of at most 0.0071.
Values may be sent and summed in bfloat16 or wider, within the bound.
A program may use at most 64 MiB of HBM per device.

```python
import math
import jax
import jax.numpy as jnp
import numpy as np
from jax import lax

D = 4096
L = 1024
H = 2048
ROW_DEV = 128
TOP = 4
EXPERTS = 8
CAP = 128
ROWS = 1024
N_EXPERT = 8


def levels(own_key, shape, cuts, least, top_value):
    def one(dim, shards_of):
        heights = jax.random.uniform(jax.random.fold_in(jax.random.fold_in(own_key, 6), dim), (shards_of,), jnp.float32, least / len(cuts), top_value / len(cuts))
        return jnp.repeat(jnp.exp(heights), shape[dim] // shards_of).reshape((-1,) + (1,) * (len(shape) - dim - 1))

    level = one(*cuts[0])
    for cut in cuts[1:]:
        level = level * one(*cut)
    return level


def shared_out(own_key, own, number, rows, count, top, most, slope):
    sequence = jax.random.permutation(own_key, count)
    packed, usual = portions_of(count, rows * top, most, slope, True), portions_of(count, rows * top, most, slope, False)
    places = jnp.arange(count)

    def named(sizes, offset_by):
        used = int((sizes > 0).sum())
        fixed = max(1, used // 4)
        passed = fixed + (places - fixed + offset_by * (used - fixed)) % max(1, count - fixed)
        return jnp.zeros((count,), jnp.int32).at[sequence[jnp.where(places < fixed, places, passed)]].set(jnp.asarray(sizes, jnp.int32))

    sizes = jnp.where(number % 4 == 0, named(packed, number // 4), named(usual, number - number // 4 - 1))
    mixed = jax.random.permutation(jax.random.fold_in(own, 3), count)
    donor, sink = mixed[0:count // 2 * 2:2], mixed[1:count // 2 * 2:2]
    slack = jnp.minimum(sizes[donor] - 1, most - sizes[sink]) // 2
    slack = jnp.where((donor == sequence[0]) | (sink == sequence[0]) | (sizes[sink] == 0), 0, jnp.maximum(slack, 0))
    passed = jax.random.randint(jax.random.fold_in(own, 4), (count // 2,), 0, 1 << 20) % (slack + 1)
    sizes = sizes.at[donor].add(-passed).at[sink].add(passed)
    items = jnp.searchsorted(jnp.cumsum(sizes), jnp.arange(rows * top), side="right").astype(jnp.int32)
    listing = items.reshape(top, rows).T
    listing = listing[jax.random.permutation(jax.random.fold_in(own, 1), rows)]
    offset_by = jax.random.randint(jax.random.fold_in(own, 2), (rows, 1), 0, top)
    return jnp.take_along_axis(listing, (jnp.arange(top)[None, :] + offset_by) % top, axis=1)


def portions_of(amount, total, most, lean, full):
    weights = [(1 << 20) // math.isqrt(standing ** lean) + 1 for standing in range(1, amount + 1)]
    largest = most if full else min(most, max(-(-total // amount), total * weights[0] // sum(weights)))
    least = 1 if total - largest >= amount - 1 else 0
    holding, spare = [largest] + [least] * (amount - 1), total - largest - least * (amount - 1)
    while spare > 0:
        free = [i for i in range(1, amount) if holding[i] < largest] or [i for i in range(1, amount) if holding[i] < most]
        whole, left = sum([weights[i] for i in free]), spare
        for i in free:
            more = min(most - holding[i], max(1, left * weights[i] // whole), spare)
            holding[i] = holding[i] + more
            spare = spare - more
    return np.array(holding)


def gaussian(rng, extent, width, reach, shards=(), held_as=jnp.bfloat16):
    entries = jax.random.normal(rng, extent, jnp.float32) * width
    if len(shards) > 0:
        entries = levels(rng, extent, shards, -0.22, 0.18) * entries
    return jnp.clip(entries, min=-reach, max=reach).astype(held_as)


def setup_inputs(seed: int = 0, part: int = 0) -> dict:
    streams_of = jax.random.split(jax.random.key(seed), 8)
    own_keys = jax.random.split(jax.random.fold_in(streams_of[7], part), 8)
    tokens = gaussian(own_keys[0], (ROWS, D), 1.0, 6.0, ((0, 8), (1, 2)))
    latent_down = gaussian(streams_of[1], (D, L), D ** -0.5, 0.09375, ((0, 2),))
    expert_gate = gaussian(streams_of[2], (EXPERTS, L, H), L ** -0.5, 0.1875, ((0, 8), (2, 2)))
    expert_up = gaussian(streams_of[3], (EXPERTS, L, H), L ** -0.5, 0.1875, ((0, 8), (2, 2)))
    expert_down = gaussian(streams_of[4], (EXPERTS, H, L), H ** -0.5, 0.125, ((0, 8), (1, 2)))
    routes_keys = jax.random.split(jax.random.fold_in(own_keys[5], 1), ROWS // ROW_DEV)
    routes_turns = jax.random.permutation(jax.random.fold_in(own_keys[5], 3), ROWS // ROW_DEV)
    routes = jax.vmap(lambda own, number: shared_out(jax.random.fold_in(own_keys[5], 2), own, number, ROW_DEV, EXPERTS, TOP, CAP, 2))(routes_keys, routes_turns).reshape((ROWS, TOP))
    gates = jnp.clip(jnp.exp(math.log(1.0) - 2.3025851 * jax.random.uniform(own_keys[6], (ROWS, TOP), jnp.float32) ** levels(own_keys[6], (ROWS, TOP), ((0, 8),), -0.2, 0.2)), 0.1, 1.0)
    return dict(tokens=tokens, latent_down=latent_down, expert_gate=expert_gate, expert_up=expert_up, expert_down=expert_down, routes=routes, gates=gates)


def slot_tables(route_rows, gate_rows):
    row_count = route_rows.shape[0]
    pick_ids = route_rows.reshape(-1)
    expert_ids = jnp.arange(EXPERTS, dtype=jnp.int32)
    onehot = (pick_ids[:, None] == expert_ids[None, :]).astype(jnp.int32)
    earlier = jnp.cumsum(onehot, axis=0) - onehot
    position = jnp.sum(earlier * onehot, axis=1).astype(jnp.int32)
    slot_ids = pick_ids * CAP + position
    all_slots = jnp.arange(EXPERTS * CAP, dtype=jnp.int32)
    slot_hits = (slot_ids[None, :] == all_slots[:, None]).astype(jnp.float32)
    slot_hits = slot_hits.reshape(EXPERTS * CAP, row_count, TOP)
    placing = jnp.sum(slot_hits, axis=2)
    mixing = jnp.sum(slot_hits * gate_rows[None, :, :], axis=2).T
    return placing, mixing


def reference(tokens, latent_down, expert_gate, expert_up, expert_down, routes, gates):
    latent = jnp.dot(tokens, latent_down, preferred_element_type=jnp.float32).astype(jnp.bfloat16)
    latent_blocks = latent.reshape(N_EXPERT, ROW_DEV, L)
    route_blocks = routes.reshape(N_EXPERT, ROW_DEV, TOP)
    gate_blocks = gates.reshape(N_EXPERT, ROW_DEV, TOP)
    placing, mixing = jax.vmap(slot_tables)(route_blocks, gate_blocks)

    def place_rows(place_table, latent_rows):
        return jnp.dot(place_table.astype(jnp.bfloat16), latent_rows, preferred_element_type=jnp.float32).astype(jnp.bfloat16)

    outgoing = jax.vmap(place_rows)(placing, latent_blocks)
    outgoing = outgoing.reshape(N_EXPERT, EXPERTS, CAP, L).transpose(1, 0, 2, 3).reshape(EXPERTS, N_EXPERT * CAP, L)

    def expert_apply(expert_items):
        slot_rows, w_gate, w_up, w_down = expert_items
        gate_part = jnp.dot(slot_rows, w_gate, preferred_element_type=jnp.float32)
        up_part = jnp.dot(slot_rows, w_up, preferred_element_type=jnp.float32)
        hidden = (jax.nn.silu(gate_part) * up_part).astype(jnp.bfloat16)
        return jnp.dot(hidden, w_down, preferred_element_type=jnp.float32).astype(jnp.bfloat16)

    expert_out = lax.map(expert_apply, (outgoing, expert_gate, expert_up, expert_down))
    expert_out = expert_out.reshape(EXPERTS, N_EXPERT, CAP, L).transpose(1, 0, 2, 3).reshape(N_EXPERT, EXPERTS * CAP, L)

    def combine_rows(mix_table, returned_rows):
        return jnp.dot(mix_table, returned_rows.astype(jnp.float32), precision=lax.Precision.HIGHEST, preferred_element_type=jnp.float32)

    mixed = jax.vmap(combine_rows)(mixing, expert_out)
    return mixed.reshape(ROWS, L).astype(jnp.bfloat16)
```

```python
import functools

import jax
import jax.numpy as jnp
from jax import lax
from jax.experimental import pallas as pl
from jax.experimental.pallas import tpu as pltpu
from jax.sharding import PartitionSpec as P

MESH = pl.DeviceIdType.MESH
F32 = jnp.float32
BF16 = jnp.bfloat16


def slot_tables(route_rows, gate_rows, devices, capacity):
    row_count, per_row = route_rows.shape
    pick_ids = route_rows.reshape(-1)
    expert_ids = jnp.arange(devices, dtype=jnp.int32)
    onehot = (pick_ids[:, None] == expert_ids[None, :]).astype(jnp.int32)
    earlier = jnp.cumsum(onehot, axis=0) - onehot
    position = jnp.sum(earlier * onehot, axis=1)
    slot_ids = pick_ids * capacity + position
    all_slots = jnp.arange(devices * capacity, dtype=jnp.int32)
    slot_hits = (slot_ids[None, :] == all_slots[:, None]).astype(jnp.float32)
    slot_hits = slot_hits.reshape(devices * capacity, row_count, per_row)
    placing = jnp.sum(slot_hits, axis=2).astype(jnp.bfloat16)
    mixing = jnp.sum(slot_hits * gate_rows[None, :, :], axis=2).T
    return (placing, mixing)


def by_slots(tokens, latent_down, expert_gate, expert_up, expert_down, routes, gates):
    devices = lax.axis_size("expert")
    row_count, per_row = routes.shape
    capacity = 2 * row_count * per_row // devices
    placing, mixing = slot_tables(routes, gates, devices, capacity)
    partial_latent = jnp.dot(tokens, latent_down, preferred_element_type=jnp.float32)
    latent = lax.psum_scatter(partial_latent, "tensor", scatter_dimension=1, tiled=True).astype(
        jnp.bfloat16
    )
    outgoing = jnp.dot(placing, latent, preferred_element_type=jnp.float32).astype(jnp.bfloat16)
    outgoing = outgoing.reshape(devices, capacity, latent.shape[1])
    slot_rows = lax.all_gather(
        lax.all_to_all(outgoing, "expert", split_axis=0, concat_axis=0, tiled=True),
        "tensor",
        axis=2,
        tiled=True,
    )
    gate_part = jnp.einsum(
        "snl,lh->snh", slot_rows, expert_gate[0], preferred_element_type=jnp.float32
    )
    up_part = jnp.einsum("snl,lh->snh", slot_rows, expert_up[0], preferred_element_type=jnp.float32)
    hidden = (jax.nn.silu(gate_part) * up_part).astype(jnp.bfloat16)
    partial_value = jnp.einsum(
        "snh,hl->snl", hidden, expert_down[0], preferred_element_type=jnp.float32
    )
    results = lax.psum_scatter(partial_value, "tensor", scatter_dimension=2, tiled=True).astype(
        jnp.bfloat16
    )
    returned = lax.all_to_all(results, "expert", split_axis=0, concat_axis=0, tiled=True)
    returned_rows = returned.reshape(devices * capacity, returned.shape[2]).astype(jnp.float32)
    mixed = jnp.dot(
        mixing, returned_rows, precision=lax.Precision.HIGHEST, preferred_element_type=jnp.float32
    )
    return mixed.astype(jnp.bfloat16)


def tile_of(size):
    return 256 if size % 256 == 0 else 128


def kernel(
    lines,
    tokens_hbm,
    down_hbm,
    wg_hbm,
    wu_hbm,
    wd_hbm,
    routes_ref,
    gates_ref,
    out_ref,
    tok,
    ld,
    wg,
    wu,
    wd,
    lat_out,
    lat_in,
    lat_own,
    table,
    x,
    hid,
    p_out,
    p_in,
    own,
    keep,
    y_out,
    y_in,
    z_out,
    z_in,
    load_sem,
    lat_sem,
    gt_send,
    gt_recv,
    az_send,
    az_recv,
    ay_send,
    ay_recv,
    ac_send,
    ac_recv,
    pc_send,
    pc_recv,
    ry_send,
    ry_recv,
    rz_send,
    rz_recv,
):
    e = lax.axis_index("expert")
    t = lax.axis_index("tensor")
    n = 2 * lines
    z, y = e // 2, lax.rem(e, 2)
    rows = tok.shape[0]
    half = out_ref.shape[1]
    other_y = 1 - y
    mate = {"tensor": 1 - t}
    beside = {"expert": z * 2 + other_y}

    def at(shift):
        return lax.rem(e + shift, n)

    barrier = pltpu.get_barrier_semaphore()
    for shift in range(1, n):
        pl.semaphore_signal(barrier, inc=1, device_id={"expert": at(shift)}, device_id_type=MESH)
    pl.semaphore_signal(barrier, inc=1, device_id=mate, device_id_type=MESH)

    mate_cols = pl.ds(pl.multiple_of((1 - t) * half, half), half)
    own_cols = pl.ds(pl.multiple_of(t * half, half), half)
    loads = [
        pltpu.make_async_copy(tokens_hbm, tok, load_sem.at[0]),
        pltpu.make_async_copy(down_hbm.at[:, mate_cols], ld.at[0], load_sem.at[1]),
        pltpu.make_async_copy(down_hbm.at[:, own_cols], ld.at[1], load_sem.at[2]),
        pltpu.make_async_copy(wg_hbm.at[0], wg, load_sem.at[3]),
        pltpu.make_async_copy(wu_hbm.at[0], wu, load_sem.at[4]),
        pltpu.make_async_copy(wd_hbm.at[0], wd, load_sem.at[5]),
    ]
    for load in loads[:3]:
        load.start()

    experts = lax.broadcasted_iota(jnp.int32, (n, rows), 0)
    weight = jnp.zeros((n, rows), F32)
    for k in range(routes_ref.shape[0]):
        weight += jnp.where(routes_ref[k : k + 1, :] == experts, gates_ref[k : k + 1, :], 0.0)
    table[e] = weight

    loads[0].wait()
    loads[1].wait()
    for load in loads[3:]:
        load.start()

    lat_out[...] = jnp.dot(tok[...], ld[0], preferred_element_type=F32)
    pl.semaphore_wait(barrier, n)

    def remote(src, dst, send, recv, where):
        return pltpu.make_async_remote_copy(
            src_ref=src,
            dst_ref=dst,
            send_sem=send,
            recv_sem=recv,
            device_id=where,
            device_id_type=MESH,
        )

    lat_copy = remote(lat_out, lat_in, lat_sem.at[0], lat_sem.at[1], mate)
    lat_copy.start()
    tables = []
    for shift in range(1, n):
        copy = remote(
            table.at[e], table.at[e], gt_send.at[shift], gt_recv.at[shift], {"expert": at(shift)}
        )
        copy.start()
        tables.append(copy)
    loads[2].wait()
    lat_own[...] = jnp.dot(tok[...], ld[1], preferred_element_type=F32)

    def block(index):
        return pl.ds(pl.multiple_of(index * rows, rows), rows)

    def line(step):
        return lax.rem(z + lines - step, lines)

    def piece(step, side):
        return x.at[t, block(line(step) * 2 + side)]

    az = [None] * lines
    ay = [None] * lines
    ac = [[None, None] for _ in range(lines)]
    for step in range(lines):
        mine = x.at[t, block(e)]
        if step:
            target = {"expert": lax.rem(z + step, lines) * 2 + y}
            az[step] = remote(mine, mine, az_send.at[step], az_recv.at[step], target)
        source = piece(step, y)
        ay[step] = remote(source, source, ay_send.at[step], ay_recv.at[step], beside)
        for place, side in enumerate((y, other_y)):
            source = piece(step, side)
            ac[step][place] = remote(
                source, source, ac_send.at[step, place], ac_recv.at[step, place], mate
            )

    lat_copy.wait_recv()
    x[t, block(e)] = (lat_own[...] + lat_in[...]).astype(BF16)
    ay[0].start()
    for step in range(1, lines):
        az[step].start()
    ac[0][0].start()

    def pass_on(step):
        az[step].wait_recv()
        ay[step].start()
        ac[step][0].start()

    def pass_over(step):
        ay[step].wait_recv()
        ac[step][1].start()

    hidden_units = wg.shape[1]

    def up(step):
        for place in range(2):
            ac[step][place].wait_recv()
        pair = pl.ds(pl.multiple_of(line(step) * 2 * rows, 2 * rows), 2 * rows)
        width = tile_of(hidden_units)

        @pl.loop(0, hidden_units // width)
        def _(j):
            cols = pl.ds(pl.multiple_of(j * width, width), width)
            item = jnp.concatenate([x[0, pair], x[1, pair]], axis=1)
            g = jnp.dot(item, wg[:, cols], preferred_element_type=F32)
            u = jnp.dot(item, wu[:, cols], preferred_element_type=F32)
            hid[:, cols] = (g / (1.0 + jnp.exp(-g)) * u).astype(BF16)

    pc = [
        remote(p_out.at[s], p_in.at[s], pc_send.at[s], pc_recv.at[s], mate) for s in range(lines)
    ]
    ry = [
        remote(y_out.at[s], y_in.at[s], ry_send.at[s], ry_recv.at[s], beside) for s in range(lines)
    ]
    rz = [None] + [
        remote(
            z_out.at[s], z_in.at[s], rz_send.at[s], rz_recv.at[s], {"expert": line(s) * 2 + y}
        )
        for s in range(1, lines)
    ]

    def down(step):
        width = tile_of(half)

        @pl.loop(0, half // width)
        def _(j):
            cols = pl.ds(pl.multiple_of((1 - t) * half + j * width, width), width)
            here = pl.ds(pl.multiple_of(j * width, width), width)
            p_out[step, :, here] = jnp.dot(
                hid[...], wd[:, cols], preferred_element_type=F32
            ).astype(BF16)

        pc[step].start()

        @pl.loop(0, half // width)
        def _(j):
            cols = pl.ds(pl.multiple_of(t * half + j * width, width), width)
            here = pl.ds(pl.multiple_of(j * width, width), width)
            own[step, :, here] = jnp.dot(hid[...], wd[:, cols], preferred_element_type=F32)

    diagonal = lax.broadcasted_iota(jnp.int32, (rows, rows), 0) == lax.broadcasted_iota(
        jnp.int32, (rows, rows), 1
    )

    def scaled(step, side):
        part = block(side)
        across = table[line(step) * 2 + side, pl.ds(e, 1), :]
        column = jnp.sum(jnp.where(diagonal, across, 0.0), axis=1, keepdims=True)
        return (own[step, part] + p_in[step, part].astype(F32)) * column

    def back_over(step):
        pc[step].wait_recv()
        y_out[step] = scaled(step, other_y).astype(BF16)
        ry[step].start()
        keep[step] = scaled(step, y)

    def back_home(step):
        ry[step].wait_recv()
        total = keep[step] + y_in[step].astype(F32)
        if step == 0:
            keep[0] = total
        else:
            z_out[step] = total.astype(BF16)
            rz[step].start()

    order = list(range(1, lines))
    pass_over(0)
    loads[3].wait()
    loads[4].wait()
    pass_on(order[0])
    up(0)
    for later in order[1:]:
        pass_on(later)
    loads[5].wait()
    down(0)
    for copy in tables:
        copy.wait_recv()
    steps = [0] + order
    for place in range(1, lines):
        pass_over(steps[place])
        up(steps[place])
        back_over(steps[place - 1])
        down(steps[place])
        back_home(steps[place - 1])
    back_over(steps[-1])
    back_home(steps[-1])

    total = keep[0]
    for step in order:
        rz[step].wait_recv()
        total += z_in[step].astype(F32)
    out_ref[...] = total.astype(BF16)

    lat_copy.wait_send()
    for copy in tables + az[1:] + ay + [c for pair in ac for c in pair] + pc + ry + rz[1:]:
        copy.wait_send()


def by_rows(tokens, latent_down, expert_gate, expert_up, expert_down, routes, gates):
    n = lax.axis_size("expert")
    lines = n // 2
    rows, features = tokens.shape
    width = latent_down.shape[1]
    half = width // 2
    units = expert_gate.shape[2]
    vmem = pl.BlockSpec(memory_space=pltpu.VMEM)
    hbm = pl.BlockSpec(memory_space=pl.ANY)
    dma = pltpu.SemaphoreType.DMA
    flops = 2 * rows * features * width + 6 * n * rows * width * units
    return pl.pallas_call(
        functools.partial(kernel, lines),
        out_shape=jax.ShapeDtypeStruct((rows, half), BF16),
        in_specs=[hbm] * 5 + [vmem] * 2,
        out_specs=vmem,
        scratch_shapes=[
            pltpu.VMEM((rows, features), BF16),
            pltpu.VMEM((2, features, half), BF16),
            pltpu.VMEM((width, units), BF16),
            pltpu.VMEM((width, units), BF16),
            pltpu.VMEM((units, width), BF16),
            pltpu.VMEM((rows, half), F32),
            pltpu.VMEM((rows, half), F32),
            pltpu.VMEM((rows, half), F32),
            pltpu.VMEM((n, n, rows), F32),
            pltpu.VMEM((2, n * rows, half), BF16),
            pltpu.VMEM((2 * rows, units), BF16),
            pltpu.VMEM((lines, 2 * rows, half), BF16),
            pltpu.VMEM((lines, 2 * rows, half), BF16),
            pltpu.VMEM((lines, 2 * rows, half), F32),
            pltpu.VMEM((lines, rows, half), F32),
            pltpu.VMEM((lines, rows, half), BF16),
            pltpu.VMEM((lines, rows, half), BF16),
            pltpu.VMEM((lines, rows, half), BF16),
            pltpu.VMEM((lines, rows, half), BF16),
            dma((6,)),
            dma((2,)),
            dma((n,)),
            dma((n,)),
            dma((lines,)),
            dma((lines,)),
            dma((lines,)),
            dma((lines,)),
            dma((lines, 2)),
            dma((lines, 2)),
            dma((lines,)),
            dma((lines,)),
            dma((lines,)),
            dma((lines,)),
            dma((lines,)),
            dma((lines,)),
        ],
        compiler_params=pltpu.CompilerParams(
            collective_id=0, has_side_effects=True, vmem_limit_bytes=48 * 1024 * 1024
        ),
        cost_estimate=pl.CostEstimate(
            flops=flops,
            bytes_accessed=2 * (rows * features + features * width + 3 * width * units),
            transcendentals=n * rows * units,
        ),
        name="latent_experts",
    )(tokens, latent_down, expert_gate, expert_up, expert_down, routes.T, gates.T)


def on_device(tokens, latent_down, expert_gate, expert_up, expert_down, routes, gates):
    devices = lax.axis_size("expert")
    rows, per_row = routes.shape
    capacity = 2 * rows * per_row // devices
    form = by_rows if capacity >= rows and devices % 2 == 0 else by_slots
    return form(tokens, latent_down, expert_gate, expert_up, expert_down, routes, gates)


def solution(mesh):
    return jax.shard_map(
        on_device,
        mesh=mesh,
        in_specs=(
            P(("group", "expert"), "tensor"),
            P("tensor", None),
            P("expert", None, "tensor"),
            P("expert", None, "tensor"),
            P("expert", "tensor", None),
            P(("group", "expert"), None),
            P(("group", "expert"), None),
        ),
        out_specs=P(("group", "expert"), "tensor"),
        check_vma=False,
    )
```

```python
import functools

import jax
import jax.numpy as jnp
from jax import lax
from jax.experimental import pallas as pl
from jax.experimental.pallas import tpu as pltpu
from jax.sharding import PartitionSpec as P

MESH = pl.DeviceIdType.MESH
F32 = jnp.float32
BF16 = jnp.bfloat16


def slot_tables(route_rows, gate_rows, devices, capacity):
    row_count, per_row = route_rows.shape
    pick_ids = route_rows.reshape(-1)
    expert_ids = jnp.arange(devices, dtype=jnp.int32)
    onehot = (pick_ids[:, None] == expert_ids[None, :]).astype(jnp.int32)
    earlier = jnp.cumsum(onehot, axis=0) - onehot
    position = jnp.sum(earlier * onehot, axis=1)
    slot_ids = pick_ids * capacity + position
    all_slots = jnp.arange(devices * capacity, dtype=jnp.int32)
    slot_hits = (slot_ids[None, :] == all_slots[:, None]).astype(jnp.float32)
    slot_hits = slot_hits.reshape(devices * capacity, row_count, per_row)
    placing = jnp.sum(slot_hits, axis=2).astype(jnp.bfloat16)
    mixing = jnp.sum(slot_hits * gate_rows[None, :, :], axis=2).T
    return (placing, mixing)


def by_slots(tokens, latent_down, expert_gate, expert_up, expert_down, routes, gates):
    devices = lax.axis_size("expert")
    row_count, per_row = routes.shape
    capacity = 2 * row_count * per_row // devices
    placing, mixing = slot_tables(routes, gates, devices, capacity)
    partial_latent = jnp.dot(tokens, latent_down, preferred_element_type=jnp.float32)
    latent = lax.psum_scatter(partial_latent, "tensor", scatter_dimension=1, tiled=True).astype(
        jnp.bfloat16
    )
    outgoing = jnp.dot(placing, latent, preferred_element_type=jnp.float32).astype(jnp.bfloat16)
    outgoing = outgoing.reshape(devices, capacity, latent.shape[1])
    slot_rows = lax.all_gather(
        lax.all_to_all(outgoing, "expert", split_axis=0, concat_axis=0, tiled=True),
        "tensor",
        axis=2,
        tiled=True,
    )
    gate_part = jnp.einsum(
        "snl,lh->snh", slot_rows, expert_gate[0], preferred_element_type=jnp.float32
    )
    up_part = jnp.einsum("snl,lh->snh", slot_rows, expert_up[0], preferred_element_type=jnp.float32)
    hidden = (jax.nn.silu(gate_part) * up_part).astype(jnp.bfloat16)
    partial_value = jnp.einsum(
        "snh,hl->snl", hidden, expert_down[0], preferred_element_type=jnp.float32
    )
    results = lax.psum_scatter(partial_value, "tensor", scatter_dimension=2, tiled=True).astype(
        jnp.bfloat16
    )
    returned = lax.all_to_all(results, "expert", split_axis=0, concat_axis=0, tiled=True)
    returned_rows = returned.reshape(devices * capacity, returned.shape[2]).astype(jnp.float32)
    mixed = jnp.dot(
        mixing, returned_rows, precision=lax.Precision.HIGHEST, preferred_element_type=jnp.float32
    )
    return mixed.astype(jnp.bfloat16)


def tile_of(size):
    return 256 if size % 256 == 0 else 128


def kernel(
    lines,
    tokens_hbm,
    down_hbm,
    wg_hbm,
    wu_hbm,
    wd_hbm,
    routes_hbm,
    gates_hbm,
    out_ref,
    routes_ref,
    gates_ref,
    tok,
    ld,
    wg,
    wu,
    wd,
    lat_out,
    lat_in,
    lat_own,
    table,
    x,
    hid,
    p_out,
    p_in,
    own,
    keep,
    y_out,
    y_in,
    z_out,
    z_in,
    load_sem,
    lat_sem,
    tz_send,
    tz_recv,
    ty_send,
    ty_recv,
    az_send,
    az_recv,
    ay_send,
    ay_recv,
    ac_send,
    ac_recv,
    pc_send,
    pc_recv,
    ry_send,
    ry_recv,
    rz_send,
    rz_recv,
):
    e = lax.axis_index("expert")
    t = lax.axis_index("tensor")
    n = 2 * lines
    z, y = e // 2, lax.rem(e, 2)
    rows = tok.shape[0]
    half = out_ref.shape[1]
    other_y = 1 - y
    mate = {"tensor": 1 - t}
    beside = {"expert": z * 2 + other_y}

    def along(step):
        return {"expert": lax.rem(z + step, lines) * 2 + y}

    partners = [along(step) for step in range(1, lines)] + [beside, mate]
    barrier = pltpu.get_barrier_semaphore()
    for partner in partners:
        pl.semaphore_signal(barrier, inc=1, device_id=partner, device_id_type=MESH)

    mate_cols = pl.ds(pl.multiple_of((1 - t) * half, half), half)
    own_cols = pl.ds(pl.multiple_of(t * half, half), half)
    loads = [
        pltpu.make_async_copy(tokens_hbm, tok, load_sem.at[0]),
        pltpu.make_async_copy(down_hbm.at[:, mate_cols], ld.at[0], load_sem.at[1]),
        pltpu.make_async_copy(down_hbm.at[:, own_cols], ld.at[1], load_sem.at[2]),
        pltpu.make_async_copy(wg_hbm.at[0], wg, load_sem.at[3]),
        pltpu.make_async_copy(wu_hbm.at[0], wu, load_sem.at[4]),
        pltpu.make_async_copy(wd_hbm.at[0], wd, load_sem.at[5]),
        pltpu.make_async_copy(routes_hbm, routes_ref, load_sem.at[6]),
        pltpu.make_async_copy(gates_hbm, gates_ref, load_sem.at[7]),
    ]
    for load in loads[6:] + loads[:3]:
        load.start()
    loads[6].wait()
    loads[7].wait()

    experts = lax.broadcasted_iota(jnp.int32, (n, rows), 0)
    weight = jnp.zeros((n, rows), F32)
    for k in range(routes_ref.shape[0]):
        weight += jnp.where(routes_ref[k : k + 1, :] == experts, gates_ref[k : k + 1, :], 0.0)
    table[e] = weight

    loads[0].wait()
    loads[1].wait()
    for load in loads[3:6]:
        load.start()

    lat_out[...] = jnp.dot(tok[...], ld[0], preferred_element_type=F32)
    pl.semaphore_wait(barrier, len(partners))

    def remote(src, dst, send, recv, where):
        return pltpu.make_async_remote_copy(
            src_ref=src,
            dst_ref=dst,
            send_sem=send,
            recv_sem=recv,
            device_id=where,
            device_id_type=MESH,
        )

    lat_copy = remote(lat_out, lat_in, lat_sem.at[0], lat_sem.at[1], mate)
    lat_copy.start()
    loads[2].wait()
    lat_own[...] = jnp.dot(tok[...], ld[1], preferred_element_type=F32)

    def block(index):
        return pl.ds(pl.multiple_of(index * rows, rows), rows)

    def line(step):
        return lax.rem(z + lines - step, lines)

    def piece(step, side):
        return x.at[t, block(line(step) * 2 + side)]

    tz = [None] * lines
    ty = [None] * lines
    az = [None] * lines
    ay = [None] * lines
    ac = [[None, None] for _ in range(lines)]
    for step in range(lines):
        mine = x.at[t, block(e)]
        if step:
            az[step] = remote(mine, mine, az_send.at[step], az_recv.at[step], along(step))
            tz[step] = remote(
                table.at[e], table.at[e], tz_send.at[step], tz_recv.at[step], along(step)
            )
        passed = table.at[line(step) * 2 + y]
        ty[step] = remote(passed, passed, ty_send.at[step], ty_recv.at[step], beside)
        source = piece(step, y)
        ay[step] = remote(source, source, ay_send.at[step], ay_recv.at[step], beside)
        for place, side in enumerate((y, other_y)):
            source = piece(step, side)
            ac[step][place] = remote(
                source, source, ac_send.at[step, place], ac_recv.at[step, place], mate
            )

    lat_copy.wait_recv()
    x[t, block(e)] = (lat_own[...] + lat_in[...]).astype(BF16)
    order = list(range(1, lines))
    ay[0].start()
    ac[0][0].start()
    for step in order:
        az[step].start()
    ty[0].start()
    for step in order:
        tz[step].start()

    def pass_on(step):
        az[step].wait_recv()
        ay[step].start()
        ac[step][0].start()
        tz[step].wait_recv()
        ty[step].start()

    def pass_over(step):
        ay[step].wait_recv()
        ac[step][1].start()
        ty[step].wait_recv()

    hidden_units = wg.shape[1]

    def up(step):
        for place in range(2):
            ac[step][place].wait_recv()
        pair = pl.ds(pl.multiple_of(line(step) * 2 * rows, 2 * rows), 2 * rows)
        width = tile_of(hidden_units)

        @pl.loop(0, hidden_units // width, unroll=True)
        def _(j):
            cols = pl.ds(pl.multiple_of(j * width, width), width)
            item = jnp.concatenate([x[0, pair], x[1, pair]], axis=1)
            g = jnp.dot(item, wg[:, cols], preferred_element_type=F32)
            u = jnp.dot(item, wu[:, cols], preferred_element_type=F32)
            hid[:, cols] = (g / (1.0 + jnp.exp(-g)) * u).astype(BF16)

    pc = [
        remote(p_out.at[s], p_in.at[s], pc_send.at[s], pc_recv.at[s], mate) for s in range(lines)
    ]
    ry = [
        remote(y_out.at[s], y_in.at[s], ry_send.at[s], ry_recv.at[s], beside) for s in range(lines)
    ]
    rz = [None] + [
        remote(
            z_out.at[s], z_in.at[s], rz_send.at[s], rz_recv.at[s], {"expert": line(s) * 2 + y}
        )
        for s in range(1, lines)
    ]

    def down(step):
        width = tile_of(half)

        @pl.loop(0, half // width, unroll=True)
        def _(j):
            cols = pl.ds(pl.multiple_of((1 - t) * half + j * width, width), width)
            here = pl.ds(pl.multiple_of(j * width, width), width)
            p_out[step, :, here] = jnp.dot(
                hid[...], wd[:, cols], preferred_element_type=F32
            ).astype(BF16)

        pc[step].start()

        @pl.loop(0, half // width, unroll=True)
        def _(j):
            cols = pl.ds(pl.multiple_of(t * half + j * width, width), width)
            here = pl.ds(pl.multiple_of(j * width, width), width)
            own[step, :, here] = jnp.dot(hid[...], wd[:, cols], preferred_element_type=F32)

    diagonal = lax.broadcasted_iota(jnp.int32, (rows, rows), 0) == lax.broadcasted_iota(
        jnp.int32, (rows, rows), 1
    )

    def scaled(step, side):
        part = block(side)
        across = table[line(step) * 2 + side, pl.ds(e, 1), :]
        column = jnp.sum(jnp.where(diagonal, across, 0.0), axis=1, keepdims=True)
        return (own[step, part] + p_in[step, part].astype(F32)) * column

    def back_over(step):
        pc[step].wait_recv()
        y_out[step] = scaled(step, other_y).astype(BF16)
        ry[step].start()
        keep[step] = scaled(step, y)

    def back_home(step):
        ry[step].wait_recv()
        total = keep[step] + y_in[step].astype(F32)
        if step == 0:
            keep[0] = total
        else:
            z_out[step] = total.astype(BF16)
            rz[step].start()

    steps = [0] + order
    pass_over(0)
    pass_on(order[0])
    loads[3].wait()
    loads[4].wait()
    up(0)
    for step in order[1:2]:
        pass_on(step)
    loads[5].wait()
    down(0)
    for place in range(1, lines):
        pass_over(steps[place])
        if place + 2 < lines:
            pass_on(steps[place + 2])
        if place > 1:
            back_home(steps[place - 2])
        back_over(steps[place - 1])
        up(steps[place])
        down(steps[place])
    if lines > 1:
        back_home(steps[-2])
    back_over(steps[-1])
    back_home(steps[-1])

    total = keep[0]
    for step in order:
        rz[step].wait_recv()
        total += z_in[step].astype(F32)
    out_ref[...] = total.astype(BF16)

    lat_copy.wait_send()
    for copy in tz[1:] + ty + az[1:] + ay + [c for pair in ac for c in pair] + pc + ry + rz[1:]:
        copy.wait_send()


def by_rows(tokens, latent_down, expert_gate, expert_up, expert_down, routes, gates):
    n = lax.axis_size("expert")
    lines = n // 2
    rows, features = tokens.shape
    width = latent_down.shape[1]
    half = width // 2
    units = expert_gate.shape[2]
    vmem = pl.BlockSpec(memory_space=pltpu.VMEM)
    hbm = pl.BlockSpec(memory_space=pltpu.HBM)
    dma = pltpu.SemaphoreType.DMA
    flops = 2 * rows * features * width + 6 * n * rows * width * units
    return pl.pallas_call(
        functools.partial(kernel, lines),
        out_shape=jax.ShapeDtypeStruct((rows, half), BF16),
        in_specs=[hbm] * 7,
        out_specs=vmem,
        scratch_shapes=[
            pltpu.VMEM(routes.shape[::-1], jnp.int32),
            pltpu.VMEM(gates.shape[::-1], F32),
            pltpu.VMEM((rows, features), BF16),
            pltpu.VMEM((2, features, half), BF16),
            pltpu.VMEM((width, units), BF16),
            pltpu.VMEM((width, units), BF16),
            pltpu.VMEM((units, width), BF16),
            pltpu.VMEM((rows, half), F32),
            pltpu.VMEM((rows, half), F32),
            pltpu.VMEM((rows, half), F32),
            pltpu.VMEM((n, n, rows), F32),
            pltpu.VMEM((2, n * rows, half), BF16),
            pltpu.VMEM((2 * rows, units), BF16),
            pltpu.VMEM((lines, 2 * rows, half), BF16),
            pltpu.VMEM((lines, 2 * rows, half), BF16),
            pltpu.VMEM((lines, 2 * rows, half), F32),
            pltpu.VMEM((lines, rows, half), F32),
            pltpu.VMEM((lines, rows, half), BF16),
            pltpu.VMEM((lines, rows, half), BF16),
            pltpu.VMEM((lines, rows, half), BF16),
            pltpu.VMEM((lines, rows, half), BF16),
            dma((8,)),
            dma((2,)),
            dma((lines,)),
            dma((lines,)),
            dma((lines,)),
            dma((lines,)),
            dma((lines,)),
            dma((lines,)),
            dma((lines,)),
            dma((lines,)),
            dma((lines, 2)),
            dma((lines, 2)),
            dma((lines,)),
            dma((lines,)),
            dma((lines,)),
            dma((lines,)),
            dma((lines,)),
            dma((lines,)),
        ],
        compiler_params=pltpu.CompilerParams(
            collective_id=0, has_side_effects=True, vmem_limit_bytes=48 * 1024 * 1024
        ),
        cost_estimate=pl.CostEstimate(
            flops=flops,
            bytes_accessed=2 * (rows * features + features * width + 3 * width * units),
            transcendentals=n * rows * units,
        ),
        name="latent_experts",
    )(tokens, latent_down, expert_gate, expert_up, expert_down, routes.T, gates.T)


def on_device(tokens, latent_down, expert_gate, expert_up, expert_down, routes, gates):
    devices = lax.axis_size("expert")
    rows, per_row = routes.shape
    capacity = 2 * rows * per_row // devices
    form = by_rows if capacity >= rows and devices % 2 == 0 else by_slots
    return form(tokens, latent_down, expert_gate, expert_up, expert_down, routes, gates)


def solution(mesh):
    return jax.shard_map(
        on_device,
        mesh=mesh,
        in_specs=(
            P(("group", "expert"), "tensor"),
            P("tensor", None),
            P("expert", None, "tensor"),
            P("expert", None, "tensor"),
            P("expert", "tensor", None),
            P(("group", "expert"), None),
            P(("group", "expert"), None),
        ),
        out_specs=P(("group", "expert"), "tensor"),
        check_vma=False,
    )
```

```python
import functools

import jax
import jax.numpy as jnp
from jax import lax
from jax.experimental import pallas as pl
from jax.experimental.pallas import tpu as pltpu
from jax.sharding import PartitionSpec as P

MESH = pl.DeviceIdType.MESH
F32 = jnp.float32
BF16 = jnp.bfloat16


def slot_tables(route_rows, gate_rows, devices, capacity):
    row_count, per_row = route_rows.shape
    pick_ids = route_rows.reshape(-1)
    expert_ids = jnp.arange(devices, dtype=jnp.int32)
    onehot = (pick_ids[:, None] == expert_ids[None, :]).astype(jnp.int32)
    earlier = jnp.cumsum(onehot, axis=0) - onehot
    position = jnp.sum(earlier * onehot, axis=1)
    slot_ids = pick_ids * capacity + position
    all_slots = jnp.arange(devices * capacity, dtype=jnp.int32)
    slot_hits = (slot_ids[None, :] == all_slots[:, None]).astype(jnp.float32)
    slot_hits = slot_hits.reshape(devices * capacity, row_count, per_row)
    placing = jnp.sum(slot_hits, axis=2).astype(jnp.bfloat16)
    mixing = jnp.sum(slot_hits * gate_rows[None, :, :], axis=2).T
    return (placing, mixing)


def by_slots(tokens, latent_down, expert_gate, expert_up, expert_down, routes, gates):
    devices = lax.axis_size("expert")
    row_count, per_row = routes.shape
    capacity = 2 * row_count * per_row // devices
    placing, mixing = slot_tables(routes, gates, devices, capacity)
    partial_latent = jnp.dot(tokens, latent_down, preferred_element_type=jnp.float32)
    latent = lax.psum_scatter(partial_latent, "tensor", scatter_dimension=1, tiled=True).astype(
        jnp.bfloat16
    )
    outgoing = jnp.dot(placing, latent, preferred_element_type=jnp.float32).astype(jnp.bfloat16)
    outgoing = outgoing.reshape(devices, capacity, latent.shape[1])
    slot_rows = lax.all_gather(
        lax.all_to_all(outgoing, "expert", split_axis=0, concat_axis=0, tiled=True),
        "tensor",
        axis=2,
        tiled=True,
    )
    gate_part = jnp.einsum(
        "snl,lh->snh", slot_rows, expert_gate[0], preferred_element_type=jnp.float32
    )
    up_part = jnp.einsum("snl,lh->snh", slot_rows, expert_up[0], preferred_element_type=jnp.float32)
    hidden = (jax.nn.silu(gate_part) * up_part).astype(jnp.bfloat16)
    partial_value = jnp.einsum(
        "snh,hl->snl", hidden, expert_down[0], preferred_element_type=jnp.float32
    )
    results = lax.psum_scatter(partial_value, "tensor", scatter_dimension=2, tiled=True).astype(
        jnp.bfloat16
    )
    returned = lax.all_to_all(results, "expert", split_axis=0, concat_axis=0, tiled=True)
    returned_rows = returned.reshape(devices * capacity, returned.shape[2]).astype(jnp.float32)
    mixed = jnp.dot(
        mixing, returned_rows, precision=lax.Precision.HIGHEST, preferred_element_type=jnp.float32
    )
    return mixed.astype(jnp.bfloat16)


def tile_of(size):
    return 256 if size % 256 == 0 else 128


def kernel(
    lines,
    tokens_hbm,
    down_hbm,
    wg_hbm,
    wu_hbm,
    wd_hbm,
    routes_hbm,
    gates_hbm,
    out_ref,
    routes_ref,
    gates_ref,
    tok,
    ld,
    wg,
    wu,
    wd,
    lat_out,
    lat_in,
    lat_own,
    table,
    x,
    hid,
    p_out,
    p_in,
    own,
    keep,
    y_out,
    y_in,
    z_out,
    z_in,
    load_sem,
    lat_sem,
    tz_send,
    tz_recv,
    ty_send,
    ty_recv,
    az_send,
    az_recv,
    ay_send,
    ay_recv,
    ac_send,
    ac_recv,
    pc_send,
    pc_recv,
    ry_send,
    ry_recv,
    rz_send,
    rz_recv,
):
    e = lax.axis_index("expert")
    t = lax.axis_index("tensor")
    n = 2 * lines
    z, y = e // 2, lax.rem(e, 2)
    rows = tok.shape[0]
    half = out_ref.shape[1]
    other_y = 1 - y
    mate = {"tensor": 1 - t}
    beside = {"expert": z * 2 + other_y}

    def along(step):
        return {"expert": lax.rem(z + step, lines) * 2 + y}

    partners = [along(step) for step in range(1, lines)] + [beside, mate]
    barrier = pltpu.get_barrier_semaphore()
    for partner in partners:
        pl.semaphore_signal(barrier, inc=1, device_id=partner, device_id_type=MESH)

    mate_cols = pl.ds(pl.multiple_of((1 - t) * half, half), half)
    own_cols = pl.ds(pl.multiple_of(t * half, half), half)
    loads = [
        pltpu.make_async_copy(tokens_hbm, tok, load_sem.at[0]),
        pltpu.make_async_copy(down_hbm.at[:, mate_cols], ld.at[0], load_sem.at[1]),
        pltpu.make_async_copy(down_hbm.at[:, own_cols], ld.at[1], load_sem.at[2]),
        pltpu.make_async_copy(wg_hbm.at[0], wg, load_sem.at[3]),
        pltpu.make_async_copy(wu_hbm.at[0], wu, load_sem.at[4]),
        pltpu.make_async_copy(wd_hbm.at[0], wd, load_sem.at[5]),
        pltpu.make_async_copy(routes_hbm, routes_ref, load_sem.at[6]),
        pltpu.make_async_copy(gates_hbm, gates_ref, load_sem.at[7]),
    ]
    for load in loads[6:] + loads[:3]:
        load.start()
    loads[6].wait()
    loads[7].wait()

    experts = lax.broadcasted_iota(jnp.int32, (n, rows), 0)
    weight = jnp.zeros((n, rows), F32)
    for k in range(routes_ref.shape[0]):
        weight += jnp.where(routes_ref[k : k + 1, :] == experts, gates_ref[k : k + 1, :], 0.0)
    table[e] = weight

    loads[0].wait()
    loads[1].wait()
    for load in loads[3:6]:
        load.start()

    lat_out[...] = jnp.dot(tok[...], ld[0], preferred_element_type=F32)
    loads[2].wait()
    lat_own[...] = jnp.dot(tok[...], ld[1], preferred_element_type=F32)
    pl.semaphore_wait(barrier, len(partners))

    def remote(src, dst, send, recv, where):
        return pltpu.make_async_remote_copy(
            src_ref=src,
            dst_ref=dst,
            send_sem=send,
            recv_sem=recv,
            device_id=where,
            device_id_type=MESH,
        )

    lat_copy = remote(lat_out, lat_in, lat_sem.at[0], lat_sem.at[1], mate)
    lat_copy.start()

    def block(index):
        return pl.ds(pl.multiple_of(index * rows, rows), rows)

    def line(step):
        return lax.rem(z + lines - step, lines)

    def piece(step, side):
        return x.at[t, block(line(step) * 2 + side)]

    tz = [None] * lines
    ty = [None] * lines
    az = [None] * lines
    ay = [None] * lines
    ac = [[None, None] for _ in range(lines)]
    for step in range(lines):
        mine = x.at[t, block(e)]
        if step:
            az[step] = remote(mine, mine, az_send.at[step], az_recv.at[step], along(step))
            tz[step] = remote(
                table.at[e], table.at[e], tz_send.at[step], tz_recv.at[step], along(step)
            )
        passed = table.at[line(step) * 2 + y]
        ty[step] = remote(passed, passed, ty_send.at[step], ty_recv.at[step], beside)
        source = piece(step, y)
        ay[step] = remote(source, source, ay_send.at[step], ay_recv.at[step], beside)
        for place, side in enumerate((y, other_y)):
            source = piece(step, side)
            ac[step][place] = remote(
                source, source, ac_send.at[step, place], ac_recv.at[step, place], mate
            )

    ty[0].start()
    for step in range(1, lines):
        tz[step].start()
    lat_copy.wait_recv()
    x[t, block(e)] = (lat_own[...] + lat_in[...]).astype(BF16)
    order = list(range(1, lines))
    ay[0].start()
    ac[0][0].start()
    for step in order:
        az[step].start()

    def pass_on(step):
        az[step].wait_recv()
        ay[step].start()
        ac[step][0].start()
        tz[step].wait_recv()
        ty[step].start()

    def pass_over(step):
        ay[step].wait_recv()
        ac[step][1].start()
        ty[step].wait_recv()

    hidden_units = wg.shape[1]

    def up(step):
        for place in range(2):
            ac[step][place].wait_recv()
        pair = pl.ds(pl.multiple_of(line(step) * 2 * rows, 2 * rows), 2 * rows)
        width = tile_of(hidden_units)

        @pl.loop(0, hidden_units // width, unroll=True)
        def _(j):
            cols = pl.ds(pl.multiple_of(j * width, width), width)
            item = jnp.concatenate([x[0, pair], x[1, pair]], axis=1)
            g = jnp.dot(item, wg[:, cols], preferred_element_type=F32)
            u = jnp.dot(item, wu[:, cols], preferred_element_type=F32)
            hid[:, cols] = (g / (1.0 + jnp.exp(-g)) * u).astype(BF16)

    pc = [
        remote(p_out.at[s], p_in.at[s], pc_send.at[s], pc_recv.at[s], mate) for s in range(lines)
    ]
    ry = [
        remote(y_out.at[s], y_in.at[s], ry_send.at[s], ry_recv.at[s], beside) for s in range(lines)
    ]
    rz = [None] + [
        remote(
            z_out.at[s], z_in.at[s], rz_send.at[s], rz_recv.at[s], {"expert": line(s) * 2 + y}
        )
        for s in range(1, lines)
    ]

    def down(step):
        width = tile_of(half)

        @pl.loop(0, half // width, unroll=True)
        def _(j):
            cols = pl.ds(pl.multiple_of((1 - t) * half + j * width, width), width)
            here = pl.ds(pl.multiple_of(j * width, width), width)
            p_out[step, :, here] = jnp.dot(
                hid[...], wd[:, cols], preferred_element_type=F32
            ).astype(BF16)

        pc[step].start()

        @pl.loop(0, half // width, unroll=True)
        def _(j):
            cols = pl.ds(pl.multiple_of(t * half + j * width, width), width)
            here = pl.ds(pl.multiple_of(j * width, width), width)
            own[step, :, here] = jnp.dot(hid[...], wd[:, cols], preferred_element_type=F32)

    diagonal = lax.broadcasted_iota(jnp.int32, (rows, rows), 0) == lax.broadcasted_iota(
        jnp.int32, (rows, rows), 1
    )

    def scaled(step, side):
        part = block(side)
        across = table[line(step) * 2 + side, pl.ds(e, 1), :]
        column = jnp.sum(jnp.where(diagonal, across, 0.0), axis=1, keepdims=True)
        return (own[step, part] + p_in[step, part].astype(F32)) * column

    def back_over(step):
        pc[step].wait_recv()
        y_out[step] = scaled(step, other_y).astype(BF16)
        ry[step].start()
        keep[step] = scaled(step, y)

    def back_home(step):
        ry[step].wait_recv()
        total = keep[step] + y_in[step].astype(F32)
        if step == 0:
            keep[0] = total
        else:
            z_out[step] = total.astype(BF16)
            rz[step].start()

    steps = [0] + order
    pass_over(0)
    pass_on(order[0])
    loads[3].wait()
    loads[4].wait()
    up(0)
    for step in order[1:2]:
        pass_on(step)
    loads[5].wait()
    down(0)
    for place in range(1, lines):
        pass_over(steps[place])
        if place + 2 < lines:
            pass_on(steps[place + 2])
        if place > 1:
            back_home(steps[place - 2])
        back_over(steps[place - 1])
        up(steps[place])
        down(steps[place])
    if lines > 1:
        back_home(steps[-2])
    back_over(steps[-1])
    back_home(steps[-1])

    total = keep[0]
    for step in order:
        rz[step].wait_recv()
        total += z_in[step].astype(F32)
    out_ref[...] = total.astype(BF16)

    lat_copy.wait_send()
    for copy in tz[1:] + ty + az[1:] + ay + [c for pair in ac for c in pair] + pc + ry + rz[1:]:
        copy.wait_send()


def by_rows(tokens, latent_down, expert_gate, expert_up, expert_down, routes, gates):
    n = lax.axis_size("expert")
    lines = n // 2
    rows, features = tokens.shape
    width = latent_down.shape[1]
    half = width // 2
    units = expert_gate.shape[2]
    vmem = pl.BlockSpec(memory_space=pltpu.VMEM)
    hbm = pl.BlockSpec(memory_space=pltpu.HBM)
    dma = pltpu.SemaphoreType.DMA
    flops = 2 * rows * features * width + 6 * n * rows * width * units
    return pl.pallas_call(
        functools.partial(kernel, lines),
        out_shape=jax.ShapeDtypeStruct((rows, half), BF16),
        in_specs=[hbm] * 7,
        out_specs=vmem,
        scratch_shapes=[
            pltpu.VMEM(routes.shape[::-1], jnp.int32),
            pltpu.VMEM(gates.shape[::-1], F32),
            pltpu.VMEM((rows, features), BF16),
            pltpu.VMEM((2, features, half), BF16),
            pltpu.VMEM((width, units), BF16),
            pltpu.VMEM((width, units), BF16),
            pltpu.VMEM((units, width), BF16),
            pltpu.VMEM((rows, half), F32),
            pltpu.VMEM((rows, half), F32),
            pltpu.VMEM((rows, half), F32),
            pltpu.VMEM((n, n, rows), F32),
            pltpu.VMEM((2, n * rows, half), BF16),
            pltpu.VMEM((2 * rows, units), BF16),
            pltpu.VMEM((lines, 2 * rows, half), BF16),
            pltpu.VMEM((lines, 2 * rows, half), BF16),
            pltpu.VMEM((lines, 2 * rows, half), F32),
            pltpu.VMEM((lines, rows, half), F32),
            pltpu.VMEM((lines, rows, half), BF16),
            pltpu.VMEM((lines, rows, half), BF16),
            pltpu.VMEM((lines, rows, half), BF16),
            pltpu.VMEM((lines, rows, half), BF16),
            dma((8,)),
            dma((2,)),
            dma((lines,)),
            dma((lines,)),
            dma((lines,)),
            dma((lines,)),
            dma((lines,)),
            dma((lines,)),
            dma((lines,)),
            dma((lines,)),
            dma((lines, 2)),
            dma((lines, 2)),
            dma((lines,)),
            dma((lines,)),
            dma((lines,)),
            dma((lines,)),
            dma((lines,)),
            dma((lines,)),
        ],
        compiler_params=pltpu.CompilerParams(
            collective_id=0, has_side_effects=True, vmem_limit_bytes=48 * 1024 * 1024
        ),
        cost_estimate=pl.CostEstimate(
            flops=flops,
            bytes_accessed=2 * (rows * features + features * width + 3 * width * units),
            transcendentals=n * rows * units,
        ),
        name="latent_experts",
    )(tokens, latent_down, expert_gate, expert_up, expert_down, routes.T, gates.T)


def on_device(tokens, latent_down, expert_gate, expert_up, expert_down, routes, gates):
    devices = lax.axis_size("expert")
    rows, per_row = routes.shape
    capacity = 2 * rows * per_row // devices
    form = by_rows if capacity >= rows and devices % 2 == 0 else by_slots
    return form(tokens, latent_down, expert_gate, expert_up, expert_down, routes, gates)


def solution(mesh):
    return jax.shard_map(
        on_device,
        mesh=mesh,
        in_specs=(
            P(("group", "expert"), "tensor"),
            P("tensor", None),
            P("expert", None, "tensor"),
            P("expert", None, "tensor"),
            P("expert", "tensor", None),
            P(("group", "expert"), None),
            P(("group", "expert"), None),
        ),
        out_specs=P(("group", "expert"), "tensor"),
        check_vma=False,
    )
```
